32 devices in a mesh: groups: 2 (over y), ctx: 4 (over z), tp: 4 (over x, core).
Axes of the slice: x: 2, y: 2, z: 4, core: 2. Of those that a mesh axis runs over, the one named last changes fastest.
Arguments:
- queries: bfloat16 [1152, 8192], P(('groups', 'ctx'), 'tp'), parts along dimension 0, may hold values from -6 to 6
- keys: bfloat16 [1152, 1024], P(('groups', 'ctx'), 'tp'), parts along dimension 0, may hold values from -6 to 6
- values: bfloat16 [1152, 1024], P(('groups', 'ctx'), 'tp'), parts along dimension 0, may hold values from -6 to 6
- residual: bfloat16 [1152, 8192], P(('groups', 'ctx'), 'tp'), parts along dimension 0, may hold values from -4 to 4
- out_weight: bfloat16 [8192, 8192], P('tp', 'ctx'), may hold values from -0.0625 to 0.0625
- value_head: bfloat16 [8192], P('tp'), may hold values from -0.5 to 0.5
- segment_ids: int32 [1152], P(('groups', 'ctx')), parts along dimension 0, may hold values from 0 to 3, as said below
- positions: int32 [1152], P(('groups', 'ctx')), parts along dimension 0, may hold values from 0 to 251, as said below
- turn_ids: int32 [1152], P(('groups', 'ctx')), parts along dimension 0, may hold values from 0 to 15, as said below
Outputs:
- hidden_out: bfloat16 [1152, 8192], P(('groups', 'ctx'), 'tp'), parts along dimension 0
- turn_means: float32 [32], P('groups'), parts along dimension 0
The draws below stay inside these ranges and needn't reach their ends.
There are 2 independent parts, one for each index of `groups`. The reference program is written for one: setup_inputs(seed, part) draws one part's arguments, and reference() takes and returns one part's arrays. A program takes and returns all parts, laid end to end along the dimension named above; an argument that names none is the same for every part. Nothing has to cross between parts.
Inputs may be any that keep to these rules, and one draw needn't show every extreme that they name: `segment_ids`: in token order (the stored order reverted) segment ids never fall; the sequence holds 4 rollouts of 36 to 252 tokens, one of exactly 252. `positions`: A row's position is its token's offset from the first token of its rollout. `turn_ids`: A row's turn id is 4 times its segment id plus how many of its rollout's three turn starts lie at or before its position; turn starts lie at positions 1 to the rollout's length minus 1 and may coincide.
All inputs are finite; a program needn't handle non-finite values.
Results may differ from the reference program's by a relative error of at most 0.013.
Values may be sent and summed in bfloat16 or wider, within the bound.
No kernel may reach another device: no remote copies, remote signals or barrier semaphores. Data moves between devices by JAX's collectives and lax.ppermute only.
A program may use at most 64 MiB of HBM per device.

```python
import math
import jax
import jax.numpy as jnp
from jax import lax

D = 8192
QUERY_HEADS = 64
KEY_VALUE_HEADS = 8
HEAD_SIZE = 128
TOK_DEV = 144
SEGS = 4
PACKED_TOKENS = 576
SEG_MEAN = 144
TURNS = 16
N_TP = 4


def layout(base_key):
    ctx_count = PACKED_TOKENS // TOK_DEV
    half_rows = TOK_DEV // 2
    row_index = jnp.arange(PACKED_TOKENS, dtype=jnp.int32)
    block_index = row_index // TOK_DEV
    inner_index = row_index % TOK_DEV
    token_of_row = jnp.where(inner_index < half_rows, block_index * half_rows + inner_index, (2 * ctx_count - 1 - block_index) * half_rows + inner_index - half_rows)
    segment_total = SEGS
    pair_total = segment_total // 2
    lengths_first = jax.random.randint(jax.random.fold_in(base_key, 1), (pair_total,), SEG_MEAN // 4, 7 * SEG_MEAN // 4 + 1)
    lengths_first = jnp.where(jnp.arange(pair_total) == 0, 7 * SEG_MEAN // 4, lengths_first)
    seg_lengths = jnp.concatenate([lengths_first, 2 * SEG_MEAN - lengths_first]).astype(jnp.int32)
    rest_order = jax.random.permutation(jax.random.fold_in(base_key, 3), segment_total - 1) + 1
    order = jnp.concatenate([jnp.zeros((1,), jnp.int32), rest_order.astype(jnp.int32)])
    seg_lengths = seg_lengths[order]
    seg_ends = jnp.cumsum(seg_lengths).astype(jnp.int32)
    seg_starts = seg_ends - seg_lengths
    token_index = jnp.arange(PACKED_TOKENS, dtype=jnp.int32)
    seg_of_token = jnp.sum((token_index[:, None] >= seg_ends[None, :]).astype(jnp.int32), axis=1)
    pos_of_token = token_index - seg_starts[seg_of_token]
    turn_cuts = jax.random.randint(jax.random.fold_in(base_key, 4), (segment_total, 3), 1, seg_lengths[:, None])
    turn_of_token = 4 * seg_of_token + jnp.sum((pos_of_token[:, None] >= turn_cuts[seg_of_token]).astype(jnp.int32), axis=1)
    return (token_of_row, seg_of_token, pos_of_token, turn_of_token)


def draw_segment_ids(base_key, part_index):
    token_of_row, seg_of_token, pos_of_token, turn_of_token = layout(base_key)
    return seg_of_token[token_of_row].astype(jnp.int32)


def draw_positions(base_key, part_index):
    token_of_row, seg_of_token, pos_of_token, turn_of_token = layout(base_key)
    return pos_of_token[token_of_row].astype(jnp.int32)


def draw_turn_ids(base_key, part_index):
    token_of_row, seg_of_token, pos_of_token, turn_of_token = layout(base_key)
    return turn_of_token[token_of_row].astype(jnp.int32)


def draw_queries(base_key, part_index):
    complete_shape = (PACKED_TOKENS, QUERY_HEADS * HEAD_SIZE)
    sampled_inputs = jax.random.truncated_normal(jax.random.fold_in(base_key, 11), -4.0, 4.0, complete_shape) * 1.5
    return sampled_inputs.astype(jnp.bfloat16)


def draw_keys(base_key, part_index):
    complete_shape = (PACKED_TOKENS, KEY_VALUE_HEADS * HEAD_SIZE)
    sampled_inputs = jax.random.truncated_normal(jax.random.fold_in(base_key, 12), -4.0, 4.0, complete_shape) * 1.5
    return sampled_inputs.astype(jnp.bfloat16)


def block_scale(key, extent, pieces, smallest, top_value):
    level = 1.0
    for dim, blocks in pieces:
        heights = jax.random.uniform(jax.random.fold_in(jax.random.fold_in(key, 6), dim), (blocks,), jnp.float32, smallest / len(pieces), top_value / len(pieces))
        level = level * jnp.repeat(jnp.exp(heights), extent[dim] // blocks).reshape((-1,) + (1,) * (len(extent) - 1 - dim))
    return level


def scatter_about(rng, dims, scale, bound, cuts=(), held_as=jnp.bfloat16):
    drawn = jax.random.normal(rng, dims, jnp.float32) * scale
    if len(cuts) > 0:
        drawn = block_scale(rng, dims, cuts, -0.22, 0.18) * drawn
    return jnp.clip(drawn, min=-bound, max=bound).astype(held_as)


def setup_inputs(seed: int = 0, part: int = 0) -> dict:
    key_of = jax.random.split(jax.random.key(seed), 10)
    part_keys = jax.random.split(jax.random.fold_in(key_of[9], part), 10)
    return {
        "queries": draw_queries(jax.random.fold_in(jax.random.fold_in(key_of[9], part), 71), part),
        "keys": draw_keys(jax.random.fold_in(jax.random.fold_in(key_of[9], part), 71), part),
        "values": scatter_about(part_keys[2], (PACKED_TOKENS, KEY_VALUE_HEADS * HEAD_SIZE), 1.0, 6.0, ((0, 4), (1, 4))),
        "residual": scatter_about(part_keys[3], (PACKED_TOKENS, D), 0.5, 4.0, ((0, 4), (1, 4))),
        "out_weight": scatter_about(key_of[4], (QUERY_HEADS * HEAD_SIZE, D), (QUERY_HEADS * HEAD_SIZE) ** -0.5, 0.0625, ((0, 4), (1, 4))),
        "value_head": scatter_about(key_of[5], (D,), (D // 64) ** -0.5, 0.5, ((0, 4),)),
        "segment_ids": draw_segment_ids(jax.random.fold_in(jax.random.fold_in(key_of[9], part), 71), part),
        "positions": draw_positions(jax.random.fold_in(jax.random.fold_in(key_of[9], part), 71), part),
        "turn_ids": draw_turn_ids(jax.random.fold_in(jax.random.fold_in(key_of[9], part), 71), part),
    }


def reference(queries, keys, values, residual, out_weight, value_head, segment_ids, positions, turn_ids):
    sequence_length = queries.shape[0]
    query_head_group = QUERY_HEADS // KEY_VALUE_HEADS
    tile_row_count = math.gcd(sequence_length, 128)
    score_scale = 1.0 / math.sqrt(HEAD_SIZE)
    key_head_rows = keys.reshape(sequence_length, KEY_VALUE_HEADS, HEAD_SIZE).astype(jnp.float32)
    value_head_rows = values.reshape(sequence_length, KEY_VALUE_HEADS, HEAD_SIZE).astype(jnp.float32)

    def one_block(block_index):
        first_row = block_index * tile_row_count
        query_tile = lax.dynamic_slice_in_dim(queries, first_row, tile_row_count, 0)
        query_tile = query_tile.reshape(tile_row_count, KEY_VALUE_HEADS, query_head_group, HEAD_SIZE).astype(jnp.float32)
        seg_block = lax.dynamic_slice_in_dim(segment_ids, first_row, tile_row_count, 0)
        pos_block = lax.dynamic_slice_in_dim(positions, first_row, tile_row_count, 0)
        allowed = (seg_block[:, None] == segment_ids[None, :]) & (positions[None, :] <= pos_block[:, None])
        scores = jnp.einsum('qhgd,khd->hgqk', query_tile, key_head_rows) * score_scale
        scores = jnp.where(allowed, scores, -1e+30)
        row_max = lax.optimization_barrier(jnp.max(scores, axis=-1, keepdims=True))
        weights = jnp.where(allowed, jnp.exp(scores - row_max), 0.0)
        denominator = lax.optimization_barrier(jnp.sum(weights, axis=-1))
        rounded = lax.optimization_barrier(weights.astype(jnp.bfloat16)).astype(jnp.float32)
        numerator = jnp.einsum('hgqk,khd->hgqd', rounded, value_head_rows)
        outcome = numerator / denominator[..., None]
        return outcome.transpose(2, 0, 1, 3).reshape(tile_row_count, QUERY_HEADS * HEAD_SIZE).astype(jnp.bfloat16)
    attention = lax.map(one_block, jnp.arange(sequence_length // tile_row_count, dtype=jnp.int32))
    attention = attention.reshape(sequence_length, QUERY_HEADS * HEAD_SIZE)
    group_cols = QUERY_HEADS * HEAD_SIZE // N_TP
    projection = jnp.zeros((sequence_length, D), jnp.float32)
    for tp_group in range(N_TP):
        lower = tp_group * group_cols
        upper = lower + group_cols
        partial_term = jnp.dot(attention[:, lower:upper], out_weight[lower:upper], preferred_element_type=jnp.float32)
        projection = projection + lax.optimization_barrier(partial_term.astype(jnp.bfloat16)).astype(jnp.float32)
    hidden_out = (residual.astype(jnp.float32) + projection).astype(jnp.bfloat16)
    token_score = jnp.dot(hidden_out, value_head, preferred_element_type=jnp.float32)
    one_hot = (turn_ids[:, None] == jnp.arange(TURNS, dtype=jnp.int32)[None, :]).astype(jnp.float32)
    turn_sum = jnp.dot(token_score, one_hot, precision=lax.Precision.HIGHEST)
    turn_count = lax.optimization_barrier(jnp.sum(one_hot, axis=0))
    turn_means = turn_sum / jnp.maximum(turn_count, 1.0)
    return (hidden_out, turn_means)
```

```python
import functools
import math

import jax
import jax.numpy as jnp
from jax import lax
from jax.experimental import pallas as pl
from jax.experimental.pallas import tpu as pltpu
from jax.sharding import PartitionSpec as P

HEAD_SIZE = 128
TURNS = 16
MASKED = -1e30


def row_tokens(index, n_ctx, tok_rows):
    half = tok_rows // 2
    row = jnp.arange(tok_rows, dtype=jnp.int32)
    return jnp.where(row < half, index * half + row, (2 * n_ctx - 2 - index) * half + row)


def attention_kernel(q_ref, kv_ref, bias_ref, out_ref, *, kv_heads, group, scale):
    bias = bias_ref[...]
    for g in range(kv_heads):
        key = kv_ref[:, g * HEAD_SIZE : (g + 1) * HEAD_SIZE]
        value = kv_ref[:, (kv_heads + g) * HEAD_SIZE : (kv_heads + g + 1) * HEAD_SIZE]
        for h in range(g * group, (g + 1) * group):
            cols = slice(h * HEAD_SIZE, (h + 1) * HEAD_SIZE)
            scores = lax.dot_general(
                q_ref[:, cols], key, (((1,), (1,)), ((), ())), preferred_element_type=jnp.float32
            )
            scores = scores * scale + bias
            weights = jnp.exp(scores - jnp.max(scores, axis=1, keepdims=True))
            denominator = jnp.sum(weights, axis=1, keepdims=True)
            numerator = jnp.dot(
                weights.astype(jnp.bfloat16), value, preferred_element_type=jnp.float32
            )
            out_ref[:, cols] = (numerator / denominator).astype(jnp.bfloat16)


def attend(queries, kv, bias):
    kv_heads = kv.shape[1] // (2 * HEAD_SIZE)
    heads = queries.shape[1] // HEAD_SIZE
    rows, keys = bias.shape
    return pl.pallas_call(
        functools.partial(
            attention_kernel,
            kv_heads=kv_heads,
            group=heads // kv_heads,
            scale=1.0 / math.sqrt(HEAD_SIZE),
        ),
        out_shape=jax.ShapeDtypeStruct(queries.shape, jnp.bfloat16),
        in_specs=[pl.BlockSpec(memory_space=pltpu.VMEM)] * 3,
        out_specs=pl.BlockSpec(memory_space=pltpu.VMEM),
        compiler_params=pltpu.CompilerParams(vmem_limit_bytes=40 * 1024 * 1024),
        cost_estimate=pl.CostEstimate(
            flops=4 * heads * rows * keys * HEAD_SIZE,
            bytes_accessed=2 * (2 * queries.size + kv.size) + 4 * bias.size,
            transcendentals=heads * rows * keys,
        ),
        name="attention",
    )(queries, kv, bias)


def butterfly_sum(x, axes, sizes):
    total = math.prod(sizes)
    if total & (total - 1):
        return lax.psum(x, axes)
    bit = 1
    while bit < total:
        x = x + lax.ppermute(x, axes, [(i, i ^ bit) for i in range(total)])
        bit *= 2
    return x


def shards(
    n_ctx,
    n_tp,
    queries,
    keys,
    values,
    residual,
    out_weight,
    value_head,
    segment_ids,
    positions,
    turn_ids,
):
    tok_rows = queries.shape[0]
    ctx = lax.axis_index("ctx")

    def ring(x, step):
        return lax.ppermute(x, "ctx", [(i, (i + step) % n_ctx) for i in range(n_ctx)])

    own_kv = jnp.concatenate([keys, values], axis=1)
    kv = jnp.concatenate([own_kv] + [ring(own_kv, s) for s in range(1, n_ctx)], axis=0)
    key_tokens = jnp.concatenate(
        [row_tokens((ctx - s) % n_ctx, n_ctx, tok_rows) for s in range(n_ctx)]
    )
    tokens = row_tokens(ctx, n_ctx, tok_rows)
    allowed = (key_tokens[None, :] <= tokens[:, None]) & (
        key_tokens[None, :] >= (tokens - positions)[:, None]
    )
    bias = jnp.where(allowed, 0.0, MASKED).astype(jnp.float32)
    piece = attend(queries, kv, bias)

    def project(rows):
        return jnp.dot(rows, out_weight, preferred_element_type=jnp.float32)

    both = ("ctx", "tp")
    if n_ctx == n_tp and n_tp & (n_tp - 1) == 0:
        summed = None
        for s in range(n_ctx):
            following = ring(piece, 1) if s + 1 < n_ctx else None
            part = project(piece)
            bit = 1
            while bit < n_tp:
                pairs = []
                for c in range(n_ctx):
                    for t in range(n_tp):
                        if (t ^ c) & bit and (t ^ c) & (bit - 1) == 0:
                            pairs.append((c * n_tp + t, c * n_tp + (t ^ bit)))
                arrived = lax.ppermute(part.astype(jnp.bfloat16), both, pairs)
                part = part + arrived.astype(jnp.float32)
                bit *= 2
            if s == 0:
                mine = lax.axis_index("tp") == ctx
                summed = jnp.where(mine, part, 0.0)
            else:
                pairs = [(c * n_tp + c, ((c - s) % n_ctx) * n_tp + c) for c in range(n_ctx)]
                summed = summed + lax.ppermute(part.astype(jnp.bfloat16), both, pairs).astype(
                    jnp.float32
                )
            piece = following
    else:
        partial_value = project(lax.all_gather(piece, "ctx", axis=0, tiled=True))
        term_rows = lax.all_to_all(
            partial_value.astype(jnp.bfloat16), "ctx", split_axis=0, concat_axis=1, tiled=True
        )
        summed = lax.psum_scatter(term_rows, "tp", scatter_dimension=1, tiled=True)
        summed = summed.astype(jnp.float32)
    hidden_out = (residual.astype(jnp.float32) + summed).astype(jnp.bfloat16)
    token_score = jnp.dot(hidden_out, value_head, preferred_element_type=jnp.float32)
    one_hot = (turn_ids[:, None] == jnp.arange(TURNS, dtype=jnp.int32)[None, :]).astype(jnp.float32)
    local_sum = jnp.dot(token_score, one_hot, precision=lax.Precision.HIGHEST)
    local_count = jnp.where(lax.axis_index("tp") == 0, jnp.sum(one_hot, axis=0), 0.0)
    totals = butterfly_sum(jnp.stack([local_sum, local_count]), both, (n_ctx, n_tp))
    turn_means = totals[0] / jnp.maximum(totals[1], 1.0)
    return (hidden_out, turn_means)


def solution(mesh):
    return jax.shard_map(
        functools.partial(shards, mesh.shape["ctx"], mesh.shape["tp"]),
        mesh=mesh,
        in_specs=(
            P(("groups", "ctx"), "tp"),
            P(("groups", "ctx"), "tp"),
            P(("groups", "ctx"), "tp"),
            P(("groups", "ctx"), "tp"),
            P("tp", "ctx"),
            P("tp"),
            P(("groups", "ctx")),
            P(("groups", "ctx")),
            P(("groups", "ctx")),
        ),
        out_specs=(P(("groups", "ctx"), "tp"), P("groups")),
        check_vma=False,
    )
```

```python
import functools
import math

import jax
import jax.numpy as jnp
from jax import lax
from jax.experimental import pallas as pl
from jax.experimental.pallas import tpu as pltpu
from jax.sharding import PartitionSpec as P

HEAD_SIZE = 128
TURNS = 16
MASKED = -1e30


def row_tokens(index, n_ctx, tok_rows):
    half = tok_rows // 2
    row = jnp.arange(tok_rows, dtype=jnp.int32)
    return jnp.where(row < half, index * half + row, (2 * n_ctx - 2 - index) * half + row)


def attention(q_ref, kv_ref, token_ref, span_ref, out_ref):
    kv_heads = kv_ref.shape[1] // (2 * HEAD_SIZE)
    group = q_ref.shape[1] // (kv_heads * HEAD_SIZE)
    scale = math.log2(math.e) / math.sqrt(HEAD_SIZE)
    token = token_ref[...]
    allowed = (token >= span_ref[:, 0:1]) & (token <= span_ref[:, 1:2])
    bias = jnp.where(allowed, 0.0, MASKED)
    for g in range(kv_heads):
        key = kv_ref[:, g * HEAD_SIZE : (g + 1) * HEAD_SIZE]
        value = kv_ref[:, (kv_heads + g) * HEAD_SIZE : (kv_heads + g + 1) * HEAD_SIZE]
        value = jnp.concatenate([value, jnp.ones_like(value)], axis=1)
        for h in range(g * group, (g + 1) * group):
            cols = slice(h * HEAD_SIZE, (h + 1) * HEAD_SIZE)
            scores = lax.dot_general(
                q_ref[:, cols], key, (((1,), (1,)), ((), ())), preferred_element_type=jnp.float32
            )
            scores = scores + bias
            weights = jnp.exp2((scores - jnp.max(scores, axis=1, keepdims=True)) * scale)
            sums = jnp.dot(weights.astype(jnp.bfloat16), value, preferred_element_type=jnp.float32)
            out_ref[:, cols] = (sums[:, :HEAD_SIZE] / sums[:, HEAD_SIZE:]).astype(jnp.bfloat16)


VMEM = pl.BlockSpec(memory_space=pltpu.VMEM)


def attend(queries, kv, tokens, span):
    rows, keys = queries.shape[0], kv.shape[0]
    return pl.pallas_call(
        attention,
        out_shape=jax.ShapeDtypeStruct(queries.shape, jnp.bfloat16),
        in_specs=[VMEM] * 4,
        out_specs=VMEM,
        compiler_params=pltpu.CompilerParams(
            vmem_limit_bytes=2**22 + 4 * (2 * queries.size + kv.size) + 32 * rows * keys
        ),
        name="attention",
    )(queries, kv, tokens, span)


def pack_kernel(key_ref, value_ref, line_ref, out_ref):
    rows, cols = key_ref.shape
    width = out_ref.shape[1]
    out_ref[:rows, :cols] = key_ref[...]
    out_ref[:rows, cols:] = value_ref[...]
    extra = out_ref.shape[0] - rows
    at = lax.broadcasted_iota(jnp.int32, (extra, width), 0)
    lines = jnp.zeros((extra, width), jnp.float32)
    for r in range(line_ref.shape[0]):
        lines = jnp.where(at == r, line_ref[r : r + 1, :].astype(jnp.float32), lines)
    out_ref[rows:, :] = lines.astype(out_ref.dtype)


def pack(keys, values, lines):
    rows, width = keys.shape[0], keys.shape[1] + values.shape[1]
    extra = lines.shape[0]
    return pl.pallas_call(
        pack_kernel,
        out_shape=jax.ShapeDtypeStruct((rows + extra + -extra % 16, width), keys.dtype),
        in_specs=[VMEM] * 3,
        out_specs=VMEM,
        name="pack",
    )(keys, values, lines)


def shards(
    n_ctx,
    n_tp,
    queries,
    keys,
    values,
    residual,
    out_weight,
    value_head,
    segment_ids,
    positions,
    turn_ids,
):
    tok_rows = queries.shape[0]
    ctx = lax.axis_index("ctx")

    def ring(x, step):
        return lax.ppermute(x, "ctx", [(i, (i + step) % n_ctx) for i in range(n_ctx)])

    width = keys.shape[1] + values.shape[1]
    per_number = -(-tok_rows // width)
    packed = pack(keys, values, jnp.pad(turn_ids, (0, per_number * width - tok_rows)).reshape(-1, width))
    with jax.named_scope("kv"):
        packed = [packed] + [ring(packed, s) for s in range(1, n_ctx)]
    kv = jnp.concatenate([block[:tok_rows] for block in packed], axis=0)
    key_tokens = jnp.concatenate(
        [row_tokens((ctx - s) % n_ctx, n_ctx, tok_rows) for s in range(n_ctx)]
    )
    tokens = row_tokens(ctx, n_ctx, tok_rows)
    span = jnp.stack([tokens - positions, tokens], axis=1)
    piece = attend(queries, kv, key_tokens[None, :], span)
    both = ("ctx", "tp")
    wide = jnp.float32

    def one_hot(turns):
        return (jnp.arange(TURNS, dtype=turns.dtype)[:, None] == turns[None, :]).astype(jnp.bfloat16)

    if n_ctx != n_tp or n_tp != 4:
        partial_value = jnp.dot(
            lax.all_gather(piece, "ctx", axis=0, tiled=True), out_weight, preferred_element_type=wide
        )
        term_rows = lax.all_to_all(
            partial_value.astype(jnp.bfloat16), "ctx", split_axis=0, concat_axis=1, tiled=True
        )
        summed = lax.psum_scatter(term_rows, "tp", scatter_dimension=1, tiled=True)
        hidden_out = (residual.astype(wide) + summed.astype(wide)).astype(jnp.bfloat16)
        token_score = jnp.dot(hidden_out, value_head, preferred_element_type=wide)
        sums = jnp.sum(one_hot(turn_ids).astype(wide) * token_score[None, :], axis=1)
        counts = jnp.sum(one_hot(turn_ids).astype(wide), axis=1)
        counts = jnp.where(lax.axis_index("tp") == 0, counts, 0.0)
        totals = lax.psum(jnp.stack([sums, counts]), both)
        return (hidden_out, totals[0] / jnp.maximum(totals[1], 1.0))

    ctx_tp = [(c, t) for c in range(n_ctx) for t in range(n_tp)]

    def send(name, x, route):
        pairs = []
        for c, t in ctx_tp:
            target = route(c, t)
            if target is not None:
                pairs.append((c * n_tp + t, target[0] % n_ctx * n_tp + target[1]))
        with jax.named_scope(name):
            return lax.ppermute(x, both, pairs)

    def add(*terms):
        return sum(term.astype(wide) for term in terms).astype(jnp.bfloat16)

    def sibling(name, x):
        return send(name, x, lambda c, t: (c, t ^ 1))

    def across(name, x, bit):
        return send(
            name, x, lambda c, t: (c, t ^ bit) if (t ^ c) & bit and not (t ^ c) & (bit - 2) else None
        )

    def to_rows(name, x, step, differ):
        return send(
            name, x, lambda c, t: (c - step, c & -2 | t & 1) if (t ^ c) & -2 == differ else None
        )

    barrier = lax.optimization_barrier
    top = n_tp // 2
    columns = out_weight.shape[1] // 2
    tp = lax.axis_index("tp")
    second = tp % 2 == 1

    head_block = send("head", value_head, lambda c, t: (t, c))
    token_score = jnp.dot(residual, value_head, preferred_element_type=wide)
    sums = jnp.sum(one_hot(turn_ids).astype(wide) * token_score[None, :], axis=1)
    turns = [block[tok_rows : tok_rows + per_number].reshape(-1)[:tok_rows] for block in packed]
    hots = [one_hot(block) for block in turns]
    counts = sum(jnp.sum(hot.astype(wide), axis=1) for hot in hots)
    through = jnp.zeros((TURNS, out_weight.shape[1]), wide)

    def project(piece):
        part = jnp.dot(piece, out_weight, preferred_element_type=wide).astype(jnp.bfloat16)
        low, high = part[:, :columns], part[:, columns:]
        return part, jnp.where(second, high, low), jnp.where(second, low, high)

    def per_turn(s, part):
        return jnp.dot(hots[s], part, preferred_element_type=wide)

    def core_sum(keep, give, pieces):
        cut = columns // pieces
        return add(
            keep,
            jnp.concatenate(
                [sibling("core", give[:, i * cut : (i + 1) * cut]) for i in range(pieces)], axis=1
            ),
        )

    def ring_on(piece):
        with jax.named_scope("heads"):
            return ring(piece, 1)

    following = ring_on(piece)
    part, keep, give = project(piece)
    through = through + per_turn(0, part)
    piece, keep, give, through = barrier((following, keep, give, through))

    following = ring_on(piece)
    first = core_sum(keep, give, 1)
    crossed = across("x", first, top)
    piece, first = barrier((piece, first))
    part, keep, give = project(piece)
    through = through + per_turn(1, part)
    piece, keep, give, crossed, through = barrier((following, keep, give, crossed, through))

    following = ring_on(piece)
    chip = core_sum(keep, give, 1)
    even = jnp.where((tp ^ ctx) & -2 == 0, add(first, crossed), 0.0)
    crossed = across("x", chip, top)
    piece, chip, even = barrier((piece, chip, even))
    part, keep, give = project(piece)
    through = through + per_turn(2, part)
    piece, keep, give, crossed, through = barrier((following, keep, give, crossed, through))

    odd = to_rows("rows1", add(chip, crossed), 1, 0)
    chip = core_sum(keep, give, 1)
    back = [to_rows("rows2", chip, 2, differ) for differ in (0, top)]
    piece, chip = barrier((piece, chip))
    part = jnp.dot(piece, out_weight, preferred_element_type=wide).astype(jnp.bfloat16)
    arrived = send("core", part, lambda c, t: (c, t ^ 1) if (t ^ c) & 1 else None)
    through = through + per_turn(3, part)
    sums = sums + jnp.sum(through * head_block.astype(wide)[None, :], axis=1)
    bit = 1
    while bit < n_tp:
        with jax.named_scope("turns_tp"):
            sums = sums + lax.ppermute(sums, "tp", [(t, t ^ bit) for t in range(n_tp)])
        bit *= 2
    chip = add(part, arrived)
    last = [
        send("rows3", chip, lambda c, t: (c + 1, c) if t ^ c == differ else None)
        for differ in (0, top)
    ]
    even = add(even, *back)
    mine = (tp ^ ctx) & 1 == 0
    other = sibling("swap", jnp.where(mine, odd, even))
    same = jnp.where(mine, even, odd)
    sums, chip = barrier((sums, chip))
    with jax.named_scope("turns_ctx"):
        sums = sum([ring(sums, step) for step in range(1, n_ctx)], sums)
    low, high = jnp.where(second, other, same), jnp.where(second, same, other)
    hidden_out = add(residual, jnp.concatenate([low, high], axis=1), *last)
    return (hidden_out, sums / jnp.maximum(counts, 1.0))


def solution(mesh):
    return jax.shard_map(
        functools.partial(shards, mesh.shape["ctx"], mesh.shape["tp"]),
        mesh=mesh,
        in_specs=(
            P(("groups", "ctx"), "tp"),
            P(("groups", "ctx"), "tp"),
            P(("groups", "ctx"), "tp"),
            P(("groups", "ctx"), "tp"),
            P("tp", "ctx"),
            P("tp"),
            P(("groups", "ctx")),
            P(("groups", "ctx")),
            P(("groups", "ctx")),
        ),
        out_specs=(P(("groups", "ctx"), "tp"), P("groups")),
        check_vma=False,
    )
```

```python
import functools
import math

import jax
import jax.numpy as jnp
from jax import lax
from jax.experimental import pallas as pl
from jax.experimental.pallas import tpu as pltpu
from jax.sharding import PartitionSpec as P

HEAD_SIZE = 128
TURNS = 16
MASKED = -1e30


def row_tokens(index, n_ctx, tok_rows):
    half = tok_rows // 2
    row = jnp.arange(tok_rows, dtype=jnp.int32)
    return jnp.where(row < half, index * half + row, (2 * n_ctx - 2 - index) * half + row)


def attention(q_ref, kv_ref, token_ref, span_ref, out_ref):
    kv_heads = kv_ref.shape[1] // (2 * HEAD_SIZE)
    group = q_ref.shape[1] // (kv_heads * HEAD_SIZE)
    scale = math.log2(math.e) / math.sqrt(HEAD_SIZE)
    token = token_ref[...]
    allowed = (token >= span_ref[:, 0:1]) & (token <= span_ref[:, 1:2])
    bias = jnp.where(allowed, 0.0, MASKED)
    for g in range(kv_heads):
        key = kv_ref[:, g * HEAD_SIZE : (g + 1) * HEAD_SIZE]
        value = kv_ref[:, (kv_heads + g) * HEAD_SIZE : (kv_heads + g + 1) * HEAD_SIZE]
        value = jnp.concatenate([value, jnp.ones_like(value)], axis=1)
        for h in range(g * group, (g + 1) * group):
            cols = slice(h * HEAD_SIZE, (h + 1) * HEAD_SIZE)
            scores = lax.dot_general(
                q_ref[:, cols], key, (((1,), (1,)), ((), ())), preferred_element_type=jnp.float32
            )
            scores = scores + bias
            weights = jnp.exp2((scores - jnp.max(scores, axis=1, keepdims=True)) * scale)
            sums = jnp.dot(weights.astype(jnp.bfloat16), value, preferred_element_type=jnp.float32)
            out_ref[:, cols] = (sums[:, :HEAD_SIZE] / sums[:, HEAD_SIZE:]).astype(jnp.bfloat16)


VMEM = pl.BlockSpec(memory_space=pltpu.VMEM)


def attend(queries, kv, tokens, span):
    rows, keys = queries.shape[0], kv.shape[0]
    return pl.pallas_call(
        attention,
        out_shape=jax.ShapeDtypeStruct(queries.shape, jnp.bfloat16),
        in_specs=[VMEM] * 4,
        out_specs=VMEM,
        compiler_params=pltpu.CompilerParams(
            vmem_limit_bytes=2**22 + 4 * (2 * queries.size + kv.size) + 32 * rows * keys
        ),
        name="attention",
    )(queries, kv, tokens, span)


def pack_kernel(key_ref, value_ref, line_ref, out_ref):
    rows, cols = key_ref.shape
    out_ref[:rows, :cols] = key_ref[...]
    out_ref[:rows, cols:] = value_ref[...]
    count, length = line_ref.shape
    extra = out_ref.shape[0] - rows
    at = lax.broadcasted_iota(jnp.int32, (extra, length), 0)
    lines = jnp.zeros((extra, length), jnp.float32)
    for r in range(count):
        lines = jnp.where(at == r, line_ref[r : r + 1, :].astype(jnp.float32), lines)
    out_ref[rows:, :] = jnp.zeros((extra, out_ref.shape[1]), out_ref.dtype)
    out_ref[rows:, :length] = lines.astype(out_ref.dtype)


def pack(keys, values, lines):
    rows, width = keys.shape[0], keys.shape[1] + values.shape[1]
    extra = lines.shape[0]
    return pl.pallas_call(
        pack_kernel,
        out_shape=jax.ShapeDtypeStruct((rows + extra + -extra % 16, width), keys.dtype),
        in_specs=[VMEM] * 3,
        out_specs=VMEM,
        name="pack",
    )(keys, values, lines)


def shards(
    n_ctx,
    n_tp,
    queries,
    keys,
    values,
    residual,
    out_weight,
    value_head,
    segment_ids,
    positions,
    turn_ids,
):
    tok_rows = queries.shape[0]
    ctx = lax.axis_index("ctx")

    def ring(x, step):
        return lax.ppermute(x, "ctx", [(i, (i + step) % n_ctx) for i in range(n_ctx)])

    width = min(tok_rows, keys.shape[1] + values.shape[1])
    per_number = -(-tok_rows // width)
    lines = jnp.pad(turn_ids, (0, per_number * width - tok_rows)).reshape(per_number, width)
    packed = pack(keys, values, lines)
    with jax.named_scope("kv"):
        packed = [packed] + [ring(packed, s) for s in range(1, n_ctx)]
    kv = jnp.concatenate([block[:tok_rows] for block in packed], axis=0)
    key_tokens = jnp.concatenate(
        [row_tokens((ctx - s) % n_ctx, n_ctx, tok_rows) for s in range(n_ctx)]
    )
    tokens = row_tokens(ctx, n_ctx, tok_rows)
    span = jnp.stack([tokens - positions, tokens], axis=1)
    piece = attend(queries, kv, key_tokens[None, :], span)
    both = ("ctx", "tp")
    wide = jnp.float32

    def one_hot(turns):
        return (jnp.arange(TURNS, dtype=turns.dtype)[:, None] == turns[None, :]).astype(jnp.bfloat16)

    if n_ctx != n_tp or n_tp != 4:
        partial_value = jnp.dot(
            lax.all_gather(piece, "ctx", axis=0, tiled=True), out_weight, preferred_element_type=wide
        )
        term_rows = lax.all_to_all(
            partial_value.astype(jnp.bfloat16), "ctx", split_axis=0, concat_axis=1, tiled=True
        )
        summed = lax.psum_scatter(term_rows, "tp", scatter_dimension=1, tiled=True)
        hidden_out = (residual.astype(wide) + summed.astype(wide)).astype(jnp.bfloat16)
        token_score = jnp.dot(hidden_out, value_head, preferred_element_type=wide)
        sums = jnp.sum(one_hot(turn_ids).astype(wide) * token_score[None, :], axis=1)
        counts = jnp.sum(one_hot(turn_ids).astype(wide), axis=1)
        counts = jnp.where(lax.axis_index("tp") == 0, counts, 0.0)
        totals = lax.psum(jnp.stack([sums, counts]), both)
        return (hidden_out, totals[0] / jnp.maximum(totals[1], 1.0))

    ctx_tp = [(c, t) for c in range(n_ctx) for t in range(n_tp)]

    def send(name, x, route):
        pairs = []
        for c, t in ctx_tp:
            target = route(c, t)
            if target is not None:
                pairs.append((c * n_tp + t, target[0] % n_ctx * n_tp + target[1]))
        with jax.named_scope(name):
            return lax.ppermute(x, both, pairs)

    def add(*terms):
        return sum(term.astype(wide) for term in terms).astype(jnp.bfloat16)

    barrier = lax.optimization_barrier
    tp = lax.axis_index("tp")
    near, own_core = (tp ^ ctx) & 2 == 0, (tp ^ ctx) & 1 == 0

    head_block = send("head", value_head, lambda c, t: (t, c))
    token_score = jnp.dot(residual, value_head, preferred_element_type=wide)
    sums = jnp.sum(one_hot(turn_ids).astype(wide) * token_score[None, :], axis=1)
    turns = [block[tok_rows : tok_rows + per_number, :width].reshape(-1)[:tok_rows] for block in packed]
    hots = [one_hot(block) for block in turns]
    counts = sum(jnp.sum(hot.astype(wide), axis=1) for hot in hots)
    through = jnp.zeros((TURNS, out_weight.shape[1]), wide)

    def project(piece):
        return jnp.dot(piece, out_weight, preferred_element_type=wide).astype(jnp.bfloat16)

    def per_turn(s, part):
        return jnp.dot(hots[s], part, preferred_element_type=wide)

    def ring_on(piece):
        with jax.named_scope("heads"):
            return ring(piece, 1)

    following = ring_on(piece)
    zero = project(piece)
    through = through + per_turn(0, zero)
    piece, zero, through = barrier((following, zero, through))

    following = ring_on(piece)
    one = project(piece)
    through = through + per_turn(1, one)
    piece, zero, one, through = barrier((following, zero, one, through))

    following = ring_on(piece)
    arrived = send("core01", jnp.where(own_core, one, zero), lambda c, t: (c, t ^ 1))
    chip = add(jnp.where(own_core, zero, one), arrived)
    piece, chip = barrier((piece, chip))
    crossed = send("x01", chip, lambda c, t: (c, t ^ 2) if (t ^ c) in (1, 2) else None)
    two = project(piece)
    through = through + per_turn(2, two)
    piece, two, chip, crossed, through = barrier((following, two, chip, crossed, through))
    settled = add(chip, crossed)

    part = project(piece)
    through = through + per_turn(3, part)
    sums = sums + jnp.sum(through * head_block.astype(wide)[None, :], axis=1)
    arrived = send("core23", jnp.where(own_core, two, part), lambda c, t: (c, t ^ 1))
    chip = add(jnp.where(own_core, part, two), arrived)
    returned = [
        send(
            "home",
            jnp.where(tp ^ ctx == 3, settled, chip),
            lambda c, t: {0: (c + 1, c), 1: (c - 2, c), 3: (c - 1, c)}.get(t ^ c),
        ),
        send("home2", chip, lambda c, t: {2: (c + 1, c), 3: (c - 2, c)}.get(t ^ c)),
    ]
    bit = 1
    while bit < n_tp:
        with jax.named_scope("turns_tp"):
            sums = sums + lax.ppermute(sums, "tp", [(t, t ^ bit) for t in range(n_tp)])
        bit *= 2
    with jax.named_scope("turns_ctx"):
        sums = sum([ring(sums, step) for step in range(1, n_ctx)], sums)
    mine = jnp.where(tp == ctx, settled, 0.0)
    return (add(residual, mine, *returned), sums / jnp.maximum(counts, 1.0))


def solution(mesh):
    return jax.shard_map(
        functools.partial(shards, mesh.shape["ctx"], mesh.shape["tp"]),
        mesh=mesh,
        in_specs=(
            P(("groups", "ctx"), "tp"),
            P(("groups", "ctx"), "tp"),
            P(("groups", "ctx"), "tp"),
            P(("groups", "ctx"), "tp"),
            P("tp", "ctx"),
            P("tp"),
            P(("groups", "ctx")),
            P(("groups", "ctx")),
            P(("groups", "ctx")),
        ),
        out_specs=(P(("groups", "ctx"), "tp"), P("groups")),
        check_vma=False,
    )
```

```python
import functools
import math

import jax
import jax.numpy as jnp
from jax import lax
from jax.experimental import pallas as pl
from jax.experimental.pallas import tpu as pltpu
from jax.sharding import PartitionSpec as P

HEAD_SIZE = 128
TURNS = 16
MASKED = -1e30


def row_tokens(index, n_ctx, tok_rows):
    half = tok_rows // 2
    row = jnp.arange(tok_rows, dtype=jnp.int32)
    return jnp.where(row < half, index * half + row, (2 * n_ctx - 2 - index) * half + row)


def attention(q_ref, kv_ref, token_ref, span_ref, out_ref):
    kv_heads = kv_ref.shape[1] // (2 * HEAD_SIZE)
    group = q_ref.shape[1] // (kv_heads * HEAD_SIZE)
    scale = math.log2(math.e) / math.sqrt(HEAD_SIZE)
    token = token_ref[...]
    allowed = (token >= span_ref[:, 0:1]) & (token <= span_ref[:, 1:2])
    bias = jnp.where(allowed, 0.0, MASKED)
    for g in range(kv_heads):
        key = kv_ref[:, g * HEAD_SIZE : (g + 1) * HEAD_SIZE]
        value = kv_ref[:, (kv_heads + g) * HEAD_SIZE : (kv_heads + g + 1) * HEAD_SIZE]
        value = jnp.concatenate([value, jnp.ones_like(value)], axis=1)
        for h in range(g * group, (g + 1) * group):
            cols = slice(h * HEAD_SIZE, (h + 1) * HEAD_SIZE)
            scores = lax.dot_general(
                q_ref[:, cols], key, (((1,), (1,)), ((), ())), preferred_element_type=jnp.float32
            )
            scores = scores + bias
            weights = jnp.exp2((scores - jnp.max(scores, axis=1, keepdims=True)) * scale)
            sums = jnp.dot(weights.astype(jnp.bfloat16), value, preferred_element_type=jnp.float32)
            out_ref[:, cols] = (sums[:, :HEAD_SIZE] / sums[:, HEAD_SIZE:]).astype(jnp.bfloat16)


VMEM = pl.BlockSpec(memory_space=pltpu.VMEM)


def attend(queries, kv, tokens, span):
    rows, keys = queries.shape[0], kv.shape[0]
    return pl.pallas_call(
        attention,
        out_shape=jax.ShapeDtypeStruct(queries.shape, jnp.bfloat16),
        in_specs=[VMEM] * 4,
        out_specs=VMEM,
        compiler_params=pltpu.CompilerParams(
            vmem_limit_bytes=2**22 + 4 * (2 * queries.size + kv.size) + 32 * rows * keys
        ),
        name="attention",
    )(queries, kv, tokens, span)


def pack_kernel(key_ref, value_ref, line_ref, out_ref):
    rows, cols = key_ref.shape
    out_ref[:rows, :cols] = key_ref[...]
    out_ref[:rows, cols:] = value_ref[...]
    count, length = line_ref.shape
    extra = out_ref.shape[0] - rows
    at = lax.broadcasted_iota(jnp.int32, (extra, length), 0)
    lines = jnp.zeros((extra, length), jnp.float32)
    for r in range(count):
        lines = jnp.where(at == r, line_ref[r : r + 1, :].astype(jnp.float32), lines)
    out_ref[rows:, :] = jnp.zeros((extra, out_ref.shape[1]), out_ref.dtype)
    out_ref[rows:, :length] = lines.astype(out_ref.dtype)


def pack(keys, values, lines):
    rows, width = keys.shape[0], keys.shape[1] + values.shape[1]
    extra = lines.shape[0]
    return pl.pallas_call(
        pack_kernel,
        out_shape=jax.ShapeDtypeStruct((rows + extra + -extra % 16, width), keys.dtype),
        in_specs=[VMEM] * 3,
        out_specs=VMEM,
        name="pack",
    )(keys, values, lines)


def shards(
    n_ctx,
    n_tp,
    queries,
    keys,
    values,
    residual,
    out_weight,
    value_head,
    segment_ids,
    positions,
    turn_ids,
):
    tok_rows = queries.shape[0]
    ctx = lax.axis_index("ctx")

    def ring(x, step):
        return lax.ppermute(x, "ctx", [(i, (i + step) % n_ctx) for i in range(n_ctx)])

    width = min(tok_rows, keys.shape[1] + values.shape[1])
    per_number = -(-tok_rows // width)
    lines = jnp.pad(turn_ids, (0, per_number * width - tok_rows)).reshape(per_number, width)
    packed = pack(keys, values, lines)
    with jax.named_scope("kv"):
        packed = [packed] + [ring(packed, s) for s in range(1, n_ctx)]
    kv = jnp.concatenate([block[:tok_rows] for block in packed], axis=0)
    key_tokens = jnp.concatenate(
        [row_tokens((ctx - s) % n_ctx, n_ctx, tok_rows) for s in range(n_ctx)]
    )
    tokens = row_tokens(ctx, n_ctx, tok_rows)
    span = jnp.stack([tokens - positions, tokens], axis=1)
    piece = attend(queries, kv, key_tokens[None, :], span)
    both = ("ctx", "tp")
    wide = jnp.float32

    def one_hot(turns):
        return (jnp.arange(TURNS, dtype=turns.dtype)[:, None] == turns[None, :]).astype(jnp.bfloat16)

    if n_ctx != n_tp or n_tp != 4:
        partial_value = jnp.dot(
            lax.all_gather(piece, "ctx", axis=0, tiled=True), out_weight, preferred_element_type=wide
        )
        term_rows = lax.all_to_all(
            partial_value.astype(jnp.bfloat16), "ctx", split_axis=0, concat_axis=1, tiled=True
        )
        summed = lax.psum_scatter(term_rows, "tp", scatter_dimension=1, tiled=True)
        hidden_out = (residual.astype(wide) + summed.astype(wide)).astype(jnp.bfloat16)
        token_score = jnp.dot(hidden_out, value_head, preferred_element_type=wide)
        sums = jnp.sum(one_hot(turn_ids).astype(wide) * token_score[None, :], axis=1)
        counts = jnp.sum(one_hot(turn_ids).astype(wide), axis=1)
        counts = jnp.where(lax.axis_index("tp") == 0, counts, 0.0)
        totals = lax.psum(jnp.stack([sums, counts]), both)
        return (hidden_out, totals[0] / jnp.maximum(totals[1], 1.0))

    ctx_tp = [(c, t) for c in range(n_ctx) for t in range(n_tp)]

    def send(name, x, route):
        pairs = []
        for c, t in ctx_tp:
            target = route(c, t)
            if target is not None:
                pairs.append((c * n_tp + t, target[0] % n_ctx * n_tp + target[1]))
        with jax.named_scope(name):
            return lax.ppermute(x, both, pairs)

    def add(*terms):
        return sum(term.astype(wide) for term in terms).astype(jnp.bfloat16)

    barrier = lax.optimization_barrier
    tp = lax.axis_index("tp")
    near, own_core = (tp ^ ctx) & 2 == 0, (tp ^ ctx) & 1 == 0

    head_block = send("head", value_head, lambda c, t: (t, c))
    piece, head_block = barrier((piece, head_block))
    token_score = jnp.dot(residual, value_head, preferred_element_type=wide)
    sums = jnp.sum(one_hot(turn_ids).astype(wide) * token_score[None, :], axis=1)
    turns = [block[tok_rows : tok_rows + per_number, :width].reshape(-1)[:tok_rows] for block in packed]
    hots = [one_hot(block) for block in turns]
    counts = sum(jnp.sum(hot.astype(wide), axis=1) for hot in hots)
    through = jnp.zeros((TURNS, out_weight.shape[1]), wide)

    def project(piece):
        return jnp.dot(piece, out_weight, preferred_element_type=wide).astype(jnp.bfloat16)

    def per_turn(s, part):
        return jnp.dot(hots[s], part, preferred_element_type=wide)

    def ring_on(piece):
        with jax.named_scope("heads"):
            return ring(piece, 1)

    following = ring_on(piece)
    zero = project(piece)
    through = through + per_turn(0, zero)
    piece, zero, through, hots, counts, sums = barrier((following, zero, through, hots, counts, sums))

    following = ring_on(piece)
    one = project(piece)
    through = through + per_turn(1, one)
    piece, zero, one, through = barrier((following, zero, one, through))

    following = ring_on(piece)
    arrived = send("core01", jnp.where(own_core, one, zero), lambda c, t: (c, t ^ 1))
    chip = add(jnp.where(own_core, zero, one), arrived)
    piece, chip = barrier((piece, chip))
    crossed = send("x01", chip, lambda c, t: (c, t ^ 2) if (t ^ c) in (1, 2) else None)
    two = project(piece)
    through = through + per_turn(2, two)
    piece, two, chip, crossed, through = barrier((following, two, chip, crossed, through))
    settled = add(chip, crossed)

    part = project(piece)
    through = through + per_turn(3, part)
    sums = sums + jnp.sum(through * head_block.astype(wide)[None, :], axis=1)
    arrived = send("core23", jnp.where(own_core, two, part), lambda c, t: (c, t ^ 1))
    chip = add(jnp.where(own_core, part, two), arrived)
    mixed = jnp.where(tp ^ ctx == 3, settled, chip)
    with jax.named_scope("turns_core"):
        sums = sums + lax.ppermute(sums, "tp", [(t, t ^ 1) for t in range(n_tp)])
    chip, mixed, sums = barrier((chip, mixed, sums))
    with jax.named_scope("turns_chip"):
        sums = sums + lax.ppermute(sums, "tp", [(t, t ^ 2) for t in range(n_tp)])
    arrived = send("x2", chip, lambda c, t: (c, t ^ 2) if t ^ c == 3 else None)
    arrived, sums = barrier((arrived, sums))
    returned = [
        send("home13", mixed, lambda c, t: {0: (c + 1, c), 3: (c - 1, c)}.get(t ^ c)),
        send(
            "home23",
            jnp.where(own_core, chip, add(chip, arrived)),
            lambda c, t: {2: (c + 1, c), 1: (c - 2, c)}.get(t ^ c),
        ),
    ]
    with jax.named_scope("turns_ctx"):
        sums = sum([ring(sums, step) for step in range(1, n_ctx)], sums)
    mine = jnp.where(tp == ctx, settled, 0.0)
    return (add(residual, mine, *returned), sums / jnp.maximum(counts, 1.0))


def solution(mesh):
    return jax.shard_map(
        functools.partial(shards, mesh.shape["ctx"], mesh.shape["tp"]),
        mesh=mesh,
        in_specs=(
            P(("groups", "ctx"), "tp"),
            P(("groups", "ctx"), "tp"),
            P(("groups", "ctx"), "tp"),
            P(("groups", "ctx"), "tp"),
            P("tp", "ctx"),
            P("tp"),
            P(("groups", "ctx")),
            P(("groups", "ctx")),
            P(("groups", "ctx")),
        ),
        out_specs=(P(("groups", "ctx"), "tp"), P("groups")),
        check_vma=False,
    )
```

```python
import functools
import math

import jax
import jax.numpy as jnp
from jax import lax
from jax.experimental import pallas as pl
from jax.experimental.pallas import tpu as pltpu
from jax.sharding import PartitionSpec as P

HEAD_SIZE = 128
TURNS = 16
MASKED = -1e30


def row_tokens(index, n_ctx, tok_rows):
    half = tok_rows // 2
    row = jnp.arange(tok_rows, dtype=jnp.int32)
    return jnp.where(row < half, index * half + row, (2 * n_ctx - 2 - index) * half + row)


def attention(q_ref, kv_ref, token_ref, span_ref, out_ref):
    kv_heads = kv_ref.shape[1] // (2 * HEAD_SIZE)
    group = q_ref.shape[1] // (kv_heads * HEAD_SIZE)
    scale = math.log2(math.e) / math.sqrt(HEAD_SIZE)
    token = token_ref[...]
    allowed = (token >= span_ref[:, 0:1]) & (token <= span_ref[:, 1:2])
    bias = jnp.where(allowed, 0.0, MASKED)
    for g in range(kv_heads):
        key = kv_ref[:, g * HEAD_SIZE : (g + 1) * HEAD_SIZE]
        value = kv_ref[:, (kv_heads + g) * HEAD_SIZE : (kv_heads + g + 1) * HEAD_SIZE]
        value = jnp.concatenate([value, jnp.ones_like(value)], axis=1)
        for h in range(g * group, (g + 1) * group):
            cols = slice(h * HEAD_SIZE, (h + 1) * HEAD_SIZE)
            scores = lax.dot_general(
                q_ref[:, cols], key, (((1,), (1,)), ((), ())), preferred_element_type=jnp.float32
            )
            scores = scores + bias
            weights = jnp.exp2((scores - jnp.max(scores, axis=1, keepdims=True)) * scale)
            sums = jnp.dot(weights.astype(jnp.bfloat16), value, preferred_element_type=jnp.float32)
            out_ref[:, cols] = (sums[:, :HEAD_SIZE] / sums[:, HEAD_SIZE:]).astype(jnp.bfloat16)


VMEM = pl.BlockSpec(memory_space=pltpu.VMEM)


def attend(queries, kv, tokens, span):
    rows, keys = queries.shape[0], kv.shape[0]
    return pl.pallas_call(
        attention,
        out_shape=jax.ShapeDtypeStruct(queries.shape, jnp.bfloat16),
        in_specs=[VMEM] * 4,
        out_specs=VMEM,
        compiler_params=pltpu.CompilerParams(
            vmem_limit_bytes=2**22 + 4 * (2 * queries.size + kv.size) + 32 * rows * keys
        ),
        name="attention",
    )(queries, kv, tokens, span)


def pack_kernel(key_ref, value_ref, line_ref, out_ref):
    rows, cols = key_ref.shape
    out_ref[:rows, :cols] = key_ref[...]
    out_ref[:rows, cols:] = value_ref[...]
    count, length = line_ref.shape
    extra = out_ref.shape[0] - rows
    at = lax.broadcasted_iota(jnp.int32, (extra, length), 0)
    lines = jnp.zeros((extra, length), jnp.float32)
    for r in range(count):
        lines = jnp.where(at == r, line_ref[r : r + 1, :].astype(jnp.float32), lines)
    out_ref[rows:, :] = jnp.zeros((extra, out_ref.shape[1]), out_ref.dtype)
    out_ref[rows:, :length] = lines.astype(out_ref.dtype)


def pack(keys, values, lines):
    rows, width = keys.shape[0], keys.shape[1] + values.shape[1]
    extra = lines.shape[0]
    return pl.pallas_call(
        pack_kernel,
        out_shape=jax.ShapeDtypeStruct((rows + extra + -extra % 16, width), keys.dtype),
        in_specs=[VMEM] * 3,
        out_specs=VMEM,
        name="pack",
    )(keys, values, lines)


def shards(
    n_ctx,
    n_tp,
    queries,
    keys,
    values,
    residual,
    out_weight,
    value_head,
    segment_ids,
    positions,
    turn_ids,
):
    tok_rows = queries.shape[0]
    ctx = lax.axis_index("ctx")

    def ring(x, step):
        return lax.ppermute(x, "ctx", [(i, (i + step) % n_ctx) for i in range(n_ctx)])

    width = min(tok_rows, keys.shape[1] + values.shape[1])
    per_number = -(-tok_rows // width)
    lines = jnp.pad(turn_ids, (0, per_number * width - tok_rows)).reshape(per_number, width)
    packed = pack(keys, values, lines)
    with jax.named_scope("kv"):
        packed = [packed] + [ring(packed, s) for s in range(1, n_ctx)]
    kv = jnp.concatenate([block[:tok_rows] for block in packed], axis=0)
    key_tokens = jnp.concatenate(
        [row_tokens((ctx - s) % n_ctx, n_ctx, tok_rows) for s in range(n_ctx)]
    )
    tokens = row_tokens(ctx, n_ctx, tok_rows)
    span = jnp.stack([tokens - positions, tokens], axis=1)
    piece = attend(queries, kv, key_tokens[None, :], span)
    both = ("ctx", "tp")
    wide = jnp.float32

    def one_hot(turns):
        return (jnp.arange(TURNS, dtype=turns.dtype)[:, None] == turns[None, :]).astype(jnp.bfloat16)

    if n_ctx != n_tp or n_tp != 4:
        partial_value = jnp.dot(
            lax.all_gather(piece, "ctx", axis=0, tiled=True), out_weight, preferred_element_type=wide
        )
        term_rows = lax.all_to_all(
            partial_value.astype(jnp.bfloat16), "ctx", split_axis=0, concat_axis=1, tiled=True
        )
        summed = lax.psum_scatter(term_rows, "tp", scatter_dimension=1, tiled=True)
        hidden_out = (residual.astype(wide) + summed.astype(wide)).astype(jnp.bfloat16)
        token_score = jnp.dot(hidden_out, value_head, preferred_element_type=wide)
        sums = jnp.sum(one_hot(turn_ids).astype(wide) * token_score[None, :], axis=1)
        counts = jnp.sum(one_hot(turn_ids).astype(wide), axis=1)
        counts = jnp.where(lax.axis_index("tp") == 0, counts, 0.0)
        totals = lax.psum(jnp.stack([sums, counts]), both)
        return (hidden_out, totals[0] / jnp.maximum(totals[1], 1.0))

    ctx_tp = [(c, t) for c in range(n_ctx) for t in range(n_tp)]

    def send(name, x, route):
        pairs = []
        for c, t in ctx_tp:
            target = route(c, t)
            if target is not None:
                pairs.append((c * n_tp + t, target[0] % n_ctx * n_tp + target[1]))
        with jax.named_scope(name):
            return lax.ppermute(x, both, pairs)

    def add(*terms):
        return sum(term.astype(wide) for term in terms).astype(jnp.bfloat16)

    barrier = lax.optimization_barrier
    tp = lax.axis_index("tp")
    near, own_core = (tp ^ ctx) & 2 == 0, (tp ^ ctx) & 1 == 0

    head_block = send("head", value_head, lambda c, t: (t, c))
    piece, head_block = barrier((piece, head_block))
    token_score = jnp.dot(residual, value_head, preferred_element_type=wide)
    sums = jnp.sum(one_hot(turn_ids).astype(wide) * token_score[None, :], axis=1)
    turns = [block[tok_rows : tok_rows + per_number, :width].reshape(-1)[:tok_rows] for block in packed]
    hots = [one_hot(block) for block in turns]
    counts = sum(jnp.sum(hot.astype(wide), axis=1) for hot in hots)
    through = jnp.zeros((TURNS, out_weight.shape[1]), wide)

    def project(piece):
        return jnp.dot(piece, out_weight, preferred_element_type=wide).astype(jnp.bfloat16)

    def per_turn(s, part):
        return jnp.dot(hots[s], part, preferred_element_type=wide)

    def ring_on(piece):
        with jax.named_scope("heads"):
            return ring(piece, 1)

    following = ring_on(piece)
    zero = project(piece)
    through = through + per_turn(0, zero)
    piece, zero, through, hots, counts, sums = barrier((following, zero, through, hots, counts, sums))

    following = ring_on(piece)
    one = project(piece)
    through = through + per_turn(1, one)
    piece, zero, one, through = barrier((following, zero, one, through))

    following = ring_on(piece)
    arrived = send("core01", jnp.where(own_core, one, zero), lambda c, t: (c, t ^ 1))
    chip = add(jnp.where(own_core, zero, one), arrived)
    piece, chip = barrier((piece, chip))
    crossed = send("x01", chip, lambda c, t: (c, t ^ 2) if (t ^ c) in (1, 2) else None)
    two = project(piece)
    through = through + per_turn(2, two)
    piece, two, chip, crossed, through = barrier((following, two, chip, crossed, through))
    settled = add(chip, crossed)

    part = project(piece)
    through = through + per_turn(3, part)
    sums = sums + jnp.sum(through * head_block.astype(wide)[None, :], axis=1)
    arrived = send("core23", jnp.where(own_core, part, two), lambda c, t: (c, t ^ 1))
    chip = add(jnp.where(own_core, two, part), arrived)
    mixed = jnp.where(tp ^ ctx == 3, settled, chip)
    with jax.named_scope("turns_core"):
        sums = sums + lax.ppermute(sums, "tp", [(t, t ^ 1) for t in range(n_tp)])
    chip, mixed, sums = barrier((chip, mixed, sums))
    with jax.named_scope("turns_chip"):
        sums = sums + lax.ppermute(sums, "tp", [(t, t ^ 2) for t in range(n_tp)])
    arrived = send("x2", chip, lambda c, t: (c, c) if t ^ c == 2 else None)
    arrived, sums = barrier((arrived, sums))
    returned = [
        send("home13", mixed, lambda c, t: {1: (c + 1, c), 3: (c - 1, c)}.get(t ^ c)),
        send(
            "home23",
            jnp.where(own_core, add(chip, arrived), chip),
            lambda c, t: {3: (c + 1, c), 0: (c - 2, c)}.get(t ^ c),
        ),
    ]
    with jax.named_scope("turns_ctx"):
        sums = sum([ring(sums, step) for step in range(1, n_ctx)], sums)
    mine = jnp.where(tp == ctx, settled, 0.0)
    return (add(residual, mine, *returned), sums / jnp.maximum(counts, 1.0))


def solution(mesh):
    return jax.shard_map(
        functools.partial(shards, mesh.shape["ctx"], mesh.shape["tp"]),
        mesh=mesh,
        in_specs=(
            P(("groups", "ctx"), "tp"),
            P(("groups", "ctx"), "tp"),
            P(("groups", "ctx"), "tp"),
            P(("groups", "ctx"), "tp"),
            P("tp", "ctx"),
            P("tp"),
            P(("groups", "ctx")),
            P(("groups", "ctx")),
            P(("groups", "ctx")),
        ),
        out_specs=(P(("groups", "ctx"), "tp"), P("groups")),
        check_vma=False,
    )
```

```python
import functools
import math

import jax
import jax.numpy as jnp
from jax import lax
from jax.experimental import pallas as pl
from jax.experimental.pallas import tpu as pltpu
from jax.sharding import PartitionSpec as P

HEAD_SIZE = 128
TURNS = 16
MASKED = -1e30


def row_tokens(index, n_ctx, tok_rows):
    half = tok_rows // 2
    row = jnp.arange(tok_rows, dtype=jnp.int32)
    return jnp.where(row < half, index * half + row, (2 * n_ctx - 2 - index) * half + row)


def attention(q_ref, kv_ref, token_ref, span_ref, out_ref):
    kv_heads = kv_ref.shape[1] // (2 * HEAD_SIZE)
    group = q_ref.shape[1] // (kv_heads * HEAD_SIZE)
    scale = math.log2(math.e) / math.sqrt(HEAD_SIZE)
    token = token_ref[...]
    allowed = (token >= span_ref[:, 0:1]) & (token <= span_ref[:, 1:2])
    bias = jnp.where(allowed, 0.0, MASKED)
    for g in range(kv_heads):
        key = kv_ref[:, g * HEAD_SIZE : (g + 1) * HEAD_SIZE]
        value = kv_ref[:, (kv_heads + g) * HEAD_SIZE : (kv_heads + g + 1) * HEAD_SIZE]
        value = jnp.concatenate([value, jnp.ones_like(value)], axis=1)
        for h in range(g * group, (g + 1) * group):
            cols = slice(h * HEAD_SIZE, (h + 1) * HEAD_SIZE)
            scores = lax.dot_general(
                q_ref[:, cols], key, (((1,), (1,)), ((), ())), preferred_element_type=jnp.float32
            )
            scores = scores + bias
            weights = jnp.exp2((scores - jnp.max(scores, axis=1, keepdims=True)) * scale)
            sums = jnp.dot(weights.astype(jnp.bfloat16), value, preferred_element_type=jnp.float32)
            out_ref[:, cols] = (sums[:, :HEAD_SIZE] / sums[:, HEAD_SIZE:]).astype(jnp.bfloat16)


VMEM = pl.BlockSpec(memory_space=pltpu.VMEM)


def attend(queries, kv, tokens, span):
    rows, keys = queries.shape[0], kv.shape[0]
    return pl.pallas_call(
        attention,
        out_shape=jax.ShapeDtypeStruct(queries.shape, jnp.bfloat16),
        in_specs=[VMEM] * 4,
        out_specs=VMEM,
        compiler_params=pltpu.CompilerParams(
            vmem_limit_bytes=2**22 + 4 * (2 * queries.size + kv.size) + 32 * rows * keys
        ),
        name="attention",
    )(queries, kv, tokens, span)


def pack_kernel(key_ref, value_ref, line_ref, out_ref):
    rows, cols = key_ref.shape
    out_ref[:rows, :cols] = key_ref[...]
    out_ref[:rows, cols:] = value_ref[...]
    count, length = line_ref.shape
    extra = out_ref.shape[0] - rows
    at = lax.broadcasted_iota(jnp.int32, (extra, length), 0)
    lines = jnp.zeros((extra, length), jnp.float32)
    for r in range(count):
        lines = jnp.where(at == r, line_ref[r : r + 1, :].astype(jnp.float32), lines)
    out_ref[rows:, :] = jnp.zeros((extra, out_ref.shape[1]), out_ref.dtype)
    out_ref[rows:, :length] = lines.astype(out_ref.dtype)


def pack(keys, values, lines):
    rows, width = keys.shape[0], keys.shape[1] + values.shape[1]
    extra = lines.shape[0]
    return pl.pallas_call(
        pack_kernel,
        out_shape=jax.ShapeDtypeStruct((rows + extra + -extra % 16, width), keys.dtype),
        in_specs=[VMEM] * 3,
        out_specs=VMEM,
        name="pack",
    )(keys, values, lines)


def shards(
    n_ctx,
    n_tp,
    queries,
    keys,
    values,
    residual,
    out_weight,
    value_head,
    segment_ids,
    positions,
    turn_ids,
):
    tok_rows = queries.shape[0]
    ctx = lax.axis_index("ctx")

    def ring(x, step):
        return lax.ppermute(x, "ctx", [(i, (i + step) % n_ctx) for i in range(n_ctx)])

    width = min(tok_rows, keys.shape[1] + values.shape[1])
    per_number = -(-tok_rows // width)
    lines = jnp.pad(turn_ids, (0, per_number * width - tok_rows)).reshape(per_number, width)
    packed = pack(keys, values, lines)
    with jax.named_scope("kv"):
        packed = [packed] + [ring(packed, s) for s in range(1, n_ctx)]
    kv = jnp.concatenate([block[:tok_rows] for block in packed], axis=0)
    key_tokens = jnp.concatenate(
        [row_tokens((ctx - s) % n_ctx, n_ctx, tok_rows) for s in range(n_ctx)]
    )
    tokens = row_tokens(ctx, n_ctx, tok_rows)
    span = jnp.stack([tokens - positions, tokens], axis=1)
    piece = attend(queries, kv, key_tokens[None, :], span)
    both = ("ctx", "tp")
    wide = jnp.float32

    def one_hot(turns):
        return (jnp.arange(TURNS, dtype=turns.dtype)[:, None] == turns[None, :]).astype(jnp.bfloat16)

    if n_ctx != n_tp or n_tp != 4:
        partial_value = jnp.dot(
            lax.all_gather(piece, "ctx", axis=0, tiled=True), out_weight, preferred_element_type=wide
        )
        term_rows = lax.all_to_all(
            partial_value.astype(jnp.bfloat16), "ctx", split_axis=0, concat_axis=1, tiled=True
        )
        summed = lax.psum_scatter(term_rows, "tp", scatter_dimension=1, tiled=True)
        hidden_out = (residual.astype(wide) + summed.astype(wide)).astype(jnp.bfloat16)
        token_score = jnp.dot(hidden_out, value_head, preferred_element_type=wide)
        sums = jnp.sum(one_hot(turn_ids).astype(wide) * token_score[None, :], axis=1)
        counts = jnp.sum(one_hot(turn_ids).astype(wide), axis=1)
        counts = jnp.where(lax.axis_index("tp") == 0, counts, 0.0)
        totals = lax.psum(jnp.stack([sums, counts]), both)
        return (hidden_out, totals[0] / jnp.maximum(totals[1], 1.0))

    ctx_tp = [(c, t) for c in range(n_ctx) for t in range(n_tp)]

    def send(name, x, route):
        pairs = []
        for c, t in ctx_tp:
            target = route(c, t)
            if target is not None:
                pairs.append((c * n_tp + t, target[0] % n_ctx * n_tp + target[1]))
        with jax.named_scope(name):
            return lax.ppermute(x, both, pairs)

    def add(*terms):
        return sum(term.astype(wide) for term in terms).astype(jnp.bfloat16)

    barrier = lax.optimization_barrier
    tp = lax.axis_index("tp")
    near, own_core = (tp ^ ctx) & 2 == 0, (tp ^ ctx) & 1 == 0

    head_block = send("head", value_head, lambda c, t: (t, c))
    piece, head_block = barrier((piece, head_block))
    token_score = jnp.dot(residual, value_head, preferred_element_type=wide)
    sums = jnp.sum(one_hot(turn_ids).astype(wide) * token_score[None, :], axis=1)
    turns = [block[tok_rows : tok_rows + per_number, :width].reshape(-1)[:tok_rows] for block in packed]
    hots = [one_hot(block) for block in turns]
    counts = sum(jnp.sum(hot.astype(wide), axis=1) for hot in hots)
    through = jnp.zeros((TURNS, out_weight.shape[1]), wide)

    def project(piece):
        return jnp.dot(piece, out_weight, preferred_element_type=wide).astype(jnp.bfloat16)

    def per_turn(s, part):
        return jnp.dot(hots[s], part, preferred_element_type=wide)

    def ring_on(piece):
        with jax.named_scope("heads"):
            return ring(piece, 1)

    following = ring_on(piece)
    zero = project(piece)
    through = through + per_turn(0, zero)
    piece, zero, through, hots, counts, sums = barrier((following, zero, through, hots, counts, sums))

    following = ring_on(piece)
    one = project(piece)
    through = through + per_turn(1, one)
    piece, zero, one, through = barrier((following, zero, one, through))

    following = ring_on(piece)
    arrived = send("core01", jnp.where(own_core, one, zero), lambda c, t: (c, t ^ 1))
    chip = add(jnp.where(own_core, zero, one), arrived)
    piece, chip = barrier((piece, chip))
    crossed = send("x01", chip, lambda c, t: (c, t ^ 2) if (t ^ c) in (1, 2) else None)
    two = project(piece)
    through = through + per_turn(2, two)
    piece, two, chip, crossed, through = barrier((following, two, chip, crossed, through))
    settled = add(chip, crossed)

    part = project(piece)
    through = through + per_turn(3, part)
    sums = sums + jnp.sum(through * head_block.astype(wide)[None, :], axis=1)
    arrived = send("core23", jnp.where(own_core, part, two), lambda c, t: (c, t ^ 1))
    chip = add(jnp.where(own_core, two, part), arrived)
    mixed = jnp.where(tp ^ ctx == 3, settled, chip)
    with jax.named_scope("turns_core"):
        sums = sums + lax.ppermute(sums, "tp", [(t, t ^ 1) for t in range(n_tp)])
    base = residual.astype(wide) + jnp.where(tp == ctx, settled, 0.0).astype(wide)
    chip, mixed, sums, base = barrier((chip, mixed, sums, base))
    with jax.named_scope("turns_chip"):
        sums = sums + lax.ppermute(sums, "tp", [(t, t ^ 2) for t in range(n_tp)])
    arrived = send("x2", chip, lambda c, t: (c, c) if t ^ c == 2 else None)
    arrived, sums = barrier((arrived, sums))
    returned = [
        send("home13", mixed, lambda c, t: {1: (c + 1, c), 3: (c - 1, c)}.get(t ^ c)),
        send(
            "home23",
            jnp.where(own_core, add(chip, arrived), chip),
            lambda c, t: {3: (c + 1, c), 0: (c - 2, c)}.get(t ^ c),
        ),
    ]
    with jax.named_scope("turns_ctx"):
        sums = sum([ring(sums, step) for step in range(1, n_ctx)], sums)
    return (add(base, *returned), sums / jnp.maximum(counts, 1.0))


def solution(mesh):
    return jax.shard_map(
        functools.partial(shards, mesh.shape["ctx"], mesh.shape["tp"]),
        mesh=mesh,
        in_specs=(
            P(("groups", "ctx"), "tp"),
            P(("groups", "ctx"), "tp"),
            P(("groups", "ctx"), "tp"),
            P(("groups", "ctx"), "tp"),
            P("tp", "ctx"),
            P("tp"),
            P(("groups", "ctx")),
            P(("groups", "ctx")),
            P(("groups", "ctx")),
        ),
        out_specs=(P(("groups", "ctx"), "tp"), P("groups")),
        check_vma=False,
    )
```

```python
import functools
import math

import jax
import jax.numpy as jnp
from jax import lax
from jax.experimental import pallas as pl
from jax.experimental.pallas import tpu as pltpu
from jax.sharding import PartitionSpec as P

HEAD_SIZE = 128
TURNS = 16
MASKED = -1e30


def row_tokens(index, n_ctx, tok_rows):
    half = tok_rows // 2
    row = jnp.arange(tok_rows, dtype=jnp.int32)
    return jnp.where(row < half, index * half + row, (2 * n_ctx - 2 - index) * half + row)


def attention(q_ref, kv_ref, token_ref, span_ref, out_ref):
    kv_heads = kv_ref.shape[1] // (2 * HEAD_SIZE)
    group = q_ref.shape[1] // (kv_heads * HEAD_SIZE)
    scale = math.log2(math.e) / math.sqrt(HEAD_SIZE)
    token = token_ref[...]
    allowed = (token >= span_ref[:, 0:1]) & (token <= span_ref[:, 1:2])
    bias = jnp.where(allowed, 0.0, MASKED)
    for g in range(kv_heads):
        key = kv_ref[:, g * HEAD_SIZE : (g + 1) * HEAD_SIZE]
        value = kv_ref[:, (kv_heads + g) * HEAD_SIZE : (kv_heads + g + 1) * HEAD_SIZE]
        value = jnp.concatenate([value, jnp.ones_like(value)], axis=1)
        for h in range(g * group, (g + 1) * group):
            cols = slice(h * HEAD_SIZE, (h + 1) * HEAD_SIZE)
            scores = lax.dot_general(
                q_ref[:, cols], key, (((1,), (1,)), ((), ())), preferred_element_type=jnp.float32
            )
            scores = scores + bias
            weights = jnp.exp2((scores - jnp.max(scores, axis=1, keepdims=True)) * scale)
            sums = jnp.dot(weights.astype(jnp.bfloat16), value, preferred_element_type=jnp.float32)
            out_ref[:, cols] = (sums[:, :HEAD_SIZE] / sums[:, HEAD_SIZE:]).astype(jnp.bfloat16)


VMEM = pl.BlockSpec(memory_space=pltpu.VMEM)


def attend(queries, kv, tokens, span):
    rows, keys = queries.shape[0], kv.shape[0]
    return pl.pallas_call(
        attention,
        out_shape=jax.ShapeDtypeStruct(queries.shape, jnp.bfloat16),
        in_specs=[VMEM] * 4,
        out_specs=VMEM,
        compiler_params=pltpu.CompilerParams(
            vmem_limit_bytes=2**22 + 4 * (2 * queries.size + kv.size) + 32 * rows * keys
        ),
        name="attention",
    )(queries, kv, tokens, span)


def pack_kernel(key_ref, value_ref, line_ref, out_ref):
    rows, cols = key_ref.shape
    out_ref[:rows, :cols] = key_ref[...]
    out_ref[:rows, cols:] = value_ref[...]
    count, length = line_ref.shape
    extra = out_ref.shape[0] - rows
    at = lax.broadcasted_iota(jnp.int32, (extra, length), 0)
    lines = jnp.zeros((extra, length), jnp.float32)
    for r in range(count):
        lines = jnp.where(at == r, line_ref[r : r + 1, :].astype(jnp.float32), lines)
    out_ref[rows:, :] = jnp.zeros((extra, out_ref.shape[1]), out_ref.dtype)
    out_ref[rows:, :length] = lines.astype(out_ref.dtype)


def pack(keys, values, lines):
    rows, width = keys.shape[0], keys.shape[1] + values.shape[1]
    extra = lines.shape[0]
    return pl.pallas_call(
        pack_kernel,
        out_shape=jax.ShapeDtypeStruct((rows + extra + -extra % 16, width), keys.dtype),
        in_specs=[VMEM] * 3,
        out_specs=VMEM,
        name="pack",
    )(keys, values, lines)


def shards(
    n_ctx,
    n_tp,
    queries,
    keys,
    values,
    residual,
    out_weight,
    value_head,
    segment_ids,
    positions,
    turn_ids,
):
    tok_rows = queries.shape[0]
    ctx = lax.axis_index("ctx")

    def ring(x, step):
        return lax.ppermute(x, "ctx", [(i, (i + step) % n_ctx) for i in range(n_ctx)])

    width = min(tok_rows, keys.shape[1] + values.shape[1])
    per_number = -(-tok_rows // width)
    lines = jnp.pad(turn_ids, (0, per_number * width - tok_rows)).reshape(per_number, width)
    packed = pack(keys, values, lines)
    swaps = n_ctx == 4
    with jax.named_scope("kv"):
        if swaps:
            packed = [packed] + [
                lax.ppermute(packed, "ctx", [(c, c ^ s) for c in range(n_ctx)])
                for s in range(1, n_ctx)
            ]
        else:
            packed = [packed] + [ring(packed, s) for s in range(1, n_ctx)]
    kv = jnp.concatenate([block[:tok_rows] for block in packed], axis=0)
    key_tokens = jnp.concatenate(
        [
            row_tokens(ctx ^ s if swaps else (ctx - s) % n_ctx, n_ctx, tok_rows)
            for s in range(n_ctx)
        ]
    )
    tokens = row_tokens(ctx, n_ctx, tok_rows)
    span = jnp.stack([tokens - positions, tokens], axis=1)
    piece = attend(queries, kv, key_tokens[None, :], span)
    both = ("ctx", "tp")
    wide = jnp.float32

    def one_hot(turns):
        return (jnp.arange(TURNS, dtype=turns.dtype)[:, None] == turns[None, :]).astype(jnp.bfloat16)

    if n_ctx != n_tp or n_tp != 4:
        partial_value = jnp.dot(
            lax.all_gather(piece, "ctx", axis=0, tiled=True), out_weight, preferred_element_type=wide
        )
        term_rows = lax.all_to_all(
            partial_value.astype(jnp.bfloat16), "ctx", split_axis=0, concat_axis=1, tiled=True
        )
        summed = lax.psum_scatter(term_rows, "tp", scatter_dimension=1, tiled=True)
        hidden_out = (residual.astype(wide) + summed.astype(wide)).astype(jnp.bfloat16)
        token_score = jnp.dot(hidden_out, value_head, preferred_element_type=wide)
        sums = jnp.sum(one_hot(turn_ids).astype(wide) * token_score[None, :], axis=1)
        counts = jnp.sum(one_hot(turn_ids).astype(wide), axis=1)
        counts = jnp.where(lax.axis_index("tp") == 0, counts, 0.0)
        totals = lax.psum(jnp.stack([sums, counts]), both)
        return (hidden_out, totals[0] / jnp.maximum(totals[1], 1.0))

    ctx_tp = [(c, t) for c in range(n_ctx) for t in range(n_tp)]

    def send(name, x, route):
        pairs = []
        for c, t in ctx_tp:
            target = route(c, t)
            if target is not None:
                pairs.append((c * n_tp + t, target[0] % n_ctx * n_tp + target[1]))
        with jax.named_scope(name):
            return lax.ppermute(x, both, pairs)

    def add(*terms):
        return sum(term.astype(wide) for term in terms).astype(jnp.bfloat16)

    barrier = lax.optimization_barrier
    tp = lax.axis_index("tp")
    near, own_core = (tp ^ ctx) & 2 == 0, (tp ^ ctx) & 1 == 0

    head_block = send("head", value_head, lambda c, t: (t, c))
    piece, head_block = barrier((piece, head_block))
    token_score = jnp.dot(residual, value_head, preferred_element_type=wide)
    sums = jnp.sum(one_hot(turn_ids).astype(wide) * token_score[None, :], axis=1)
    turns = [block[tok_rows : tok_rows + per_number, :width].reshape(-1)[:tok_rows] for block in packed]
    odd = ctx % 2 == 1
    turns[1], turns[3] = jnp.where(odd, turns[1], turns[3]), jnp.where(odd, turns[3], turns[1])
    hots = [one_hot(block) for block in turns]
    counts = sum(jnp.sum(hot.astype(wide), axis=1) for hot in hots)
    through = jnp.zeros((TURNS, out_weight.shape[1]), wide)

    def project(piece):
        return jnp.dot(piece, out_weight, preferred_element_type=wide).astype(jnp.bfloat16)

    def per_turn(s, part):
        return jnp.dot(hots[s], part, preferred_element_type=wide)

    def ring_on(piece):
        with jax.named_scope("heads"):
            return ring(piece, 1)

    following = ring_on(piece)
    zero = project(piece)
    through = through + per_turn(0, zero)
    piece, zero, through, hots, counts, sums = barrier((following, zero, through, hots, counts, sums))

    following = ring_on(piece)
    one = project(piece)
    through = through + per_turn(1, one)
    piece, zero, one, through = barrier((following, zero, one, through))

    following = ring_on(piece)
    arrived = send("core01", jnp.where(own_core, one, zero), lambda c, t: (c, t ^ 1))
    chip = add(jnp.where(own_core, zero, one), arrived)
    piece, chip = barrier((piece, chip))
    crossed = send("x01", chip, lambda c, t: (c, t ^ 2) if (t ^ c) in (1, 2) else None)
    two = project(piece)
    through = through + per_turn(2, two)
    piece, two, chip, crossed, through = barrier((following, two, chip, crossed, through))
    settled = add(chip, crossed)

    part = project(piece)
    through = through + per_turn(3, part)
    sums = sums + jnp.sum(through * head_block.astype(wide)[None, :], axis=1)
    arrived = send("core23", jnp.where(own_core, part, two), lambda c, t: (c, t ^ 1))
    chip = add(jnp.where(own_core, two, part), arrived)
    mixed = jnp.where(tp ^ ctx == 3, settled, chip)
    with jax.named_scope("turns_core"):
        sums = sums + lax.ppermute(sums, "tp", [(t, t ^ 1) for t in range(n_tp)])
    base = residual.astype(wide) + jnp.where(tp == ctx, settled, 0.0).astype(wide)
    chip, mixed, sums, base = barrier((chip, mixed, sums, base))
    with jax.named_scope("turns_chip"):
        sums = sums + lax.ppermute(sums, "tp", [(t, t ^ 2) for t in range(n_tp)])
    arrived = send("x2", chip, lambda c, t: (c, c) if t ^ c == 2 else None)
    arrived, sums = barrier((arrived, sums))
    returned = [
        send("home13", mixed, lambda c, t: {1: (c + 1, c), 3: (c - 1, c)}.get(t ^ c)),
        send(
            "home23",
            jnp.where(own_core, add(chip, arrived), chip),
            lambda c, t: {3: (c + 1, c), 0: (c - 2, c)}.get(t ^ c),
        ),
    ]
    with jax.named_scope("turns_ctx"):
        sums = sum([ring(sums, step) for step in range(1, n_ctx)], sums)
    return (add(base, *returned), sums / jnp.maximum(counts, 1.0))


def solution(mesh):
    return jax.shard_map(
        functools.partial(shards, mesh.shape["ctx"], mesh.shape["tp"]),
        mesh=mesh,
        in_specs=(
            P(("groups", "ctx"), "tp"),
            P(("groups", "ctx"), "tp"),
            P(("groups", "ctx"), "tp"),
            P(("groups", "ctx"), "tp"),
            P("tp", "ctx"),
            P("tp"),
            P(("groups", "ctx")),
            P(("groups", "ctx")),
            P(("groups", "ctx")),
        ),
        out_specs=(P(("groups", "ctx"), "tp"), P("groups")),
        check_vma=False,
    )
```

```python
import functools
import math

import jax
import jax.numpy as jnp
from jax import lax
from jax.experimental import pallas as pl
from jax.experimental.pallas import tpu as pltpu
from jax.sharding import PartitionSpec as P

HEAD_SIZE = 128
TURNS = 16
MASKED = -1e30


def row_tokens(index, n_ctx, tok_rows):
    half = tok_rows // 2
    row = jnp.arange(tok_rows, dtype=jnp.int32)
    return jnp.where(row < half, index * half + row, (2 * n_ctx - 2 - index) * half + row)


def attention(q_ref, kv_ref, token_ref, span_ref, out_ref):
    kv_heads = kv_ref.shape[1] // (2 * HEAD_SIZE)
    group = q_ref.shape[1] // (kv_heads * HEAD_SIZE)
    scale = math.log2(math.e) / math.sqrt(HEAD_SIZE)
    token = token_ref[...]
    allowed = (token >= span_ref[:, 0:1]) & (token <= span_ref[:, 1:2])
    bias = jnp.where(allowed, 0.0, MASKED)
    for g in range(kv_heads):
        key = kv_ref[:, g * HEAD_SIZE : (g + 1) * HEAD_SIZE]
        value = kv_ref[:, (kv_heads + g) * HEAD_SIZE : (kv_heads + g + 1) * HEAD_SIZE]
        value = jnp.concatenate([value, jnp.ones_like(value)], axis=1)
        for h in range(g * group, (g + 1) * group):
            cols = slice(h * HEAD_SIZE, (h + 1) * HEAD_SIZE)
            scores = lax.dot_general(
                q_ref[:, cols], key, (((1,), (1,)), ((), ())), preferred_element_type=jnp.float32
            )
            scores = scores + bias
            weights = jnp.exp2((scores - jnp.max(scores, axis=1, keepdims=True)) * scale)
            sums = jnp.dot(weights.astype(jnp.bfloat16), value, preferred_element_type=jnp.float32)
            out_ref[:, cols] = (sums[:, :HEAD_SIZE] / sums[:, HEAD_SIZE:]).astype(jnp.bfloat16)


VMEM = pl.BlockSpec(memory_space=pltpu.VMEM)


def attend(queries, kv, tokens, span):
    rows, keys = queries.shape[0], kv.shape[0]
    return pl.pallas_call(
        attention,
        out_shape=jax.ShapeDtypeStruct(queries.shape, jnp.bfloat16),
        in_specs=[VMEM] * 4,
        out_specs=VMEM,
        compiler_params=pltpu.CompilerParams(
            vmem_limit_bytes=2**22 + 4 * (2 * queries.size + kv.size) + 32 * rows * keys
        ),
        name="attention",
    )(queries, kv, tokens, span)


def pack_kernel(key_ref, value_ref, line_ref, out_ref):
    rows, cols = key_ref.shape
    out_ref[:rows, :cols] = key_ref[...]
    out_ref[:rows, cols:] = value_ref[...]
    count, length = line_ref.shape
    extra = out_ref.shape[0] - rows
    at = lax.broadcasted_iota(jnp.int32, (extra, length), 0)
    lines = jnp.zeros((extra, length), jnp.float32)
    for r in range(count):
        lines = jnp.where(at == r, line_ref[r : r + 1, :].astype(jnp.float32), lines)
    out_ref[rows:, :] = jnp.zeros((extra, out_ref.shape[1]), out_ref.dtype)
    out_ref[rows:, :length] = lines.astype(out_ref.dtype)


def pack(keys, values, lines):
    rows, width = keys.shape[0], keys.shape[1] + values.shape[1]
    extra = lines.shape[0]
    return pl.pallas_call(
        pack_kernel,
        out_shape=jax.ShapeDtypeStruct((rows + extra + -extra % 16, width), keys.dtype),
        in_specs=[VMEM] * 3,
        out_specs=VMEM,
        name="pack",
    )(keys, values, lines)


def shards(
    n_ctx,
    n_tp,
    queries,
    keys,
    values,
    residual,
    out_weight,
    value_head,
    segment_ids,
    positions,
    turn_ids,
):
    tok_rows = queries.shape[0]
    ctx = lax.axis_index("ctx")

    def ring(x, step):
        return lax.ppermute(x, "ctx", [(i, (i + step) % n_ctx) for i in range(n_ctx)])

    width = min(tok_rows, keys.shape[1] + values.shape[1])
    per_number = -(-tok_rows // width)
    lines = jnp.pad(turn_ids, (0, per_number * width - tok_rows)).reshape(per_number, width)
    packed = pack(keys, values, lines)
    swaps = n_ctx == 4
    with jax.named_scope("kv"):
        if swaps:
            packed = [packed] + [
                lax.ppermute(packed, "ctx", [(c, c ^ s) for c in range(n_ctx)])
                for s in range(1, n_ctx)
            ]
        else:
            packed = [packed] + [ring(packed, s) for s in range(1, n_ctx)]
    kv = jnp.concatenate([block[:tok_rows] for block in packed], axis=0)
    key_tokens = jnp.concatenate(
        [
            row_tokens(ctx ^ s if swaps else (ctx - s) % n_ctx, n_ctx, tok_rows)
            for s in range(n_ctx)
        ]
    )
    tokens = row_tokens(ctx, n_ctx, tok_rows)
    span = jnp.stack([tokens - positions, tokens], axis=1)
    piece = attend(queries, kv, key_tokens[None, :], span)
    both = ("ctx", "tp")
    wide = jnp.float32

    def one_hot(turns):
        return (jnp.arange(TURNS, dtype=turns.dtype)[:, None] == turns[None, :]).astype(jnp.bfloat16)

    if n_ctx != n_tp or n_tp != 4:
        partial_value = jnp.dot(
            lax.all_gather(piece, "ctx", axis=0, tiled=True), out_weight, preferred_element_type=wide
        )
        term_rows = lax.all_to_all(
            partial_value.astype(jnp.bfloat16), "ctx", split_axis=0, concat_axis=1, tiled=True
        )
        summed = lax.psum_scatter(term_rows, "tp", scatter_dimension=1, tiled=True)
        hidden_out = (residual.astype(wide) + summed.astype(wide)).astype(jnp.bfloat16)
        token_score = jnp.dot(hidden_out, value_head, preferred_element_type=wide)
        sums = jnp.sum(one_hot(turn_ids).astype(wide) * token_score[None, :], axis=1)
        counts = jnp.sum(one_hot(turn_ids).astype(wide), axis=1)
        counts = jnp.where(lax.axis_index("tp") == 0, counts, 0.0)
        totals = lax.psum(jnp.stack([sums, counts]), both)
        return (hidden_out, totals[0] / jnp.maximum(totals[1], 1.0))

    ctx_tp = [(c, t) for c in range(n_ctx) for t in range(n_tp)]

    def send(name, x, route):
        pairs = []
        for c, t in ctx_tp:
            target = route(c, t)
            if target is not None:
                pairs.append((c * n_tp + t, target[0] % n_ctx * n_tp + target[1]))
        with jax.named_scope(name):
            return lax.ppermute(x, both, pairs)

    def add(*terms):
        return sum(term.astype(wide) for term in terms).astype(jnp.bfloat16)

    barrier = lax.optimization_barrier
    tp = lax.axis_index("tp")
    near, own_core = (tp ^ ctx) & 2 == 0, (tp ^ ctx) & 1 == 0

    head_block = send("head", value_head, lambda c, t: (t, c))
    piece, head_block = barrier((piece, head_block))
    token_score = jnp.dot(residual, value_head, preferred_element_type=wide)
    sums = jnp.sum(one_hot(turn_ids).astype(wide) * token_score[None, :], axis=1)
    turns = [block[tok_rows : tok_rows + per_number, :width].reshape(-1)[:tok_rows] for block in packed]
    odd = ctx % 2 == 1
    turns[1], turns[3] = jnp.where(odd, turns[1], turns[3]), jnp.where(odd, turns[3], turns[1])
    hots = [one_hot(block) for block in turns]
    counts = sum(jnp.sum(hot.astype(wide), axis=1) for hot in hots)
    through = jnp.zeros((TURNS, out_weight.shape[1]), wide)

    def project(piece):
        return jnp.dot(piece, out_weight, preferred_element_type=wide).astype(jnp.bfloat16)

    def per_turn(s, part):
        return jnp.dot(hots[s], part, preferred_element_type=wide)

    def ring_on(piece):
        with jax.named_scope("heads"):
            return ring(piece, 1)

    following = ring_on(piece)
    zero = project(piece)
    through = through + per_turn(0, zero)
    piece, zero, through, hots, counts, sums = barrier((following, zero, through, hots, counts, sums))

    following = ring_on(piece)
    one = project(piece)
    through = through + per_turn(1, one)
    piece, zero, one, through = barrier((following, zero, one, through))

    following = ring_on(piece)
    arrived = send("core01", jnp.where(own_core, one, zero), lambda c, t: (c, t ^ 1))
    chip = add(jnp.where(own_core, zero, one), arrived)
    piece, chip = barrier((piece, chip))
    crossed = send("x01", chip, lambda c, t: (c, t ^ 2) if (t ^ c) in (1, 2) else None)
    two = project(piece)
    through = through + per_turn(2, two)
    piece, two, chip, crossed, through = barrier((following, two, chip, crossed, through))
    settled = add(chip, crossed)

    part = project(piece)
    through = through + per_turn(3, part)
    sums = sums + jnp.sum(through * head_block.astype(wide)[None, :], axis=1)
    arrived = send("core23", jnp.where(own_core, part, two), lambda c, t: (c, t ^ 1))
    chip = add(jnp.where(own_core, two, part), arrived)
    mixed = jnp.where(tp ^ ctx == 3, settled, chip)
    with jax.named_scope("turns_core"):
        sums = sums + lax.ppermute(sums, "tp", [(t, t ^ 1) for t in range(n_tp)])
    base = residual.astype(wide) + jnp.where(tp == ctx, settled, 0.0).astype(wide)
    chip, mixed, sums, base = barrier((chip, mixed, sums, base))
    with jax.named_scope("turns_chip"):
        sums = sums + lax.ppermute(sums, "tp", [(t, t ^ 2) for t in range(n_tp)])
    arrived = send("x2", chip, lambda c, t: (c, c) if t ^ c == 2 else None)
    arrived, sums = barrier((arrived, sums))
    returned = [
        send("home13", mixed, lambda c, t: {1: (c + 1, c), 3: (c - 1, c)}.get(t ^ c)),
        send(
            "home23",
            jnp.where(own_core, add(chip, arrived), chip),
            lambda c, t: {3: (c + 1, c), 0: (c - 2, c)}.get(t ^ c),
        ),
    ]
    with jax.named_scope("turns_ctx"):
        swapped = [
            lax.ppermute(sums, "ctx", [(c, c ^ s) for c in range(n_ctx)]) for s in range(1, n_ctx)
        ]
        sums = (sums + swapped[0]) + (swapped[1] + swapped[2])
    return (add(base, *returned), sums / jnp.maximum(counts, 1.0))


def solution(mesh):
    return jax.shard_map(
        functools.partial(shards, mesh.shape["ctx"], mesh.shape["tp"]),
        mesh=mesh,
        in_specs=(
            P(("groups", "ctx"), "tp"),
            P(("groups", "ctx"), "tp"),
            P(("groups", "ctx"), "tp"),
            P(("groups", "ctx"), "tp"),
            P("tp", "ctx"),
            P("tp"),
            P(("groups", "ctx")),
            P(("groups", "ctx")),
            P(("groups", "ctx")),
        ),
        out_specs=(P(("groups", "ctx"), "tp"), P("groups")),
        check_vma=False,
    )
```
